32 devices in a mesh: section: 2 (over y), wide: 4 (over z), narrow: 4 (over x, core).
Axes of the slice: x: 2, y: 2, z: 4, core: 2. Of those that a mesh axis runs over, the one named last changes fastest.
Arguments:
- saved_inputs: bfloat16 [2, 512, 8192], P('section', None, 'narrow'), may hold values from -6 to 6
- upstream: bfloat16 [512, 8192], P('wide', 'narrow'), may hold values from -6 to 6
- up_weight: bfloat16 [2, 8192, 16384], P('section', 'narrow', 'wide'), may hold values from -0.0625 to 0.0625
- down_weight: bfloat16 [2, 16384, 8192], P('section', 'wide', 'narrow'), may hold values from -0.046875 to 0.046875
Outputs:
- boundary_grads: bfloat16 [2, 512, 8192], P('section', 'wide', 'narrow')
- up_grads: bfloat16 [2, 8192, 16384], P('section', 'narrow', 'wide')
- down_grads: bfloat16 [2, 16384, 8192], P('section', 'wide', 'narrow')
The draws below stay inside these ranges and needn't reach their ends.
All inputs are finite; a program needn't handle non-finite values.
Results may differ from the reference program's by a relative error of at most 0.028.
Values may be sent and summed in bfloat16 or wider, within the bound.
A program may use at most 192 MiB of HBM per device.

```python
import jax
import jax.numpy as jnp

D = 8192
FF = 16384
TOKENS = 512


def block_scale(own_key, dims, pieces, smallest, largest):
    def one(position, shards_of):
        heights = jax.random.uniform(jax.random.fold_in(jax.random.fold_in(own_key, 6), position), (shards_of,), jnp.float32, smallest / len(pieces), largest / len(pieces))
        return jnp.repeat(jnp.exp(heights), dims[position] // shards_of).reshape((-1,) + (1,) * (len(dims) - position - 1))

    gain = one(*pieces[0])
    for cut in pieces[1:]:
        gain = gain * one(*cut)
    return gain


def gaussian(rng, shape, deviation, limit, split=(), kind=jnp.bfloat16):
    drawn = deviation * jax.random.normal(rng, shape, jnp.float32)
    if split:
        drawn = drawn * block_scale(rng, shape, split, -0.22, 0.18)
    return jnp.clip(drawn, -limit, limit).astype(kind)


def setup_inputs(seed: int = 0) -> dict:
    streams_of = jax.random.split(jax.random.key(seed), 5)
    return {
        "saved_inputs": gaussian(streams_of[0], (2, TOKENS, D), 1.0, 6.0, ((0, 2), (2, 4))),
        "upstream": gaussian(streams_of[1], (TOKENS, D), 1.0, 6.0, ((0, 4), (1, 4))),
        "up_weight": gaussian(streams_of[2], (2, D, FF), D ** -0.5, 0.0625, ((0, 2), (1, 4), (2, 4))),
        "down_weight": gaussian(streams_of[3], (2, FF, D), FF ** -0.5, 0.046875, ((0, 2), (1, 4), (2, 4))),
    }


gelu_scale = 0.7978845608028654
cubic_term = 0.044715


def gelu_parts(pre_act):
    inner = jnp.tanh(gelu_scale * (pre_act + cubic_term * pre_act * pre_act * pre_act))
    act_value = 0.5 * pre_act * (1.0 + inner)
    slopes = 0.5 * (1.0 + inner) + 0.5 * pre_act * (1.0 - inner * inner) * gelu_scale * (1.0 + 3.0 * cubic_term * pre_act * pre_act)
    return act_value, slopes


def layer_back(incoming, saved_rows, w_up, w_down):
    pre_act = jnp.dot(saved_rows, w_up, preferred_element_type=jnp.float32)
    act_value, slopes = gelu_parts(pre_act)
    hidden = act_value.astype(jnp.bfloat16)
    grad_down = jnp.dot(hidden.T, incoming, preferred_element_type=jnp.float32).astype(jnp.bfloat16)
    back_grad = jnp.dot(incoming, w_down.T, preferred_element_type=jnp.float32)
    slope_grad = (back_grad * slopes).astype(jnp.bfloat16)
    grad_up = jnp.dot(saved_rows.T, slope_grad, preferred_element_type=jnp.float32).astype(jnp.bfloat16)
    summed = jnp.dot(slope_grad, w_up.T, preferred_element_type=jnp.float32)
    grad_in = (incoming.astype(jnp.float32) + summed).astype(jnp.bfloat16)
    return grad_in, grad_up, grad_down


def reference(saved_inputs, upstream, up_weight, down_weight):
    upper_in, upper_up, upper_down = layer_back(upstream, saved_inputs[1], up_weight[1], down_weight[1])
    lower_in, lower_up, lower_down = layer_back(upper_in, saved_inputs[0], up_weight[0], down_weight[0])
    return (jnp.stack([lower_in, upper_in]), jnp.stack([lower_up, upper_up]), jnp.stack([lower_down, upper_down]))
```

```python
import jax
import jax.numpy as jnp
from jax import lax
from jax.sharding import PartitionSpec as P

gelu_scale = 0.7978845608028654
cubic_term = 0.044715
CHUNK_ROWS = 32


def shifted(block, axis, distance):
    size = lax.axis_size(axis)
    return lax.ppermute(block, axis, [(i, (i + distance) % size) for i in range(size)])


def from_partner(block):
    size = lax.axis_size("narrow")
    return lax.ppermute(block, "narrow", [(i, i ^ 1) for i in range(size)])


def gelu_parts(pre_act):
    inner = jnp.tanh(gelu_scale * (pre_act + cubic_term * pre_act * pre_act * pre_act))
    act_value = 0.5 * pre_act * (1.0 + inner)
    slopes = 0.5 * (1.0 + inner) + 0.5 * pre_act * (1.0 - inner * inner) * gelu_scale * (
        1.0 + 3.0 * cubic_term * pre_act * pre_act
    )
    return (act_value, slopes)


def contract_rows(first_op, second_op):
    return lax.dot_general(
        first_op, second_op, (((0,), (0,)), ((), ())), preferred_element_type=jnp.float32
    )


def contract_cols(first_op, second_op):
    return lax.dot_general(
        first_op, second_op, (((1,), (1,)), ((), ())), preferred_element_type=jnp.float32
    )


def sum_half(part, is_odd):
    half = part.shape[1] // 2
    low, high = part[:, :half], part[:, half:]
    got = from_partner(jnp.where(is_odd, low, high))
    mine = jnp.where(is_odd, high, low)
    chip = (mine.astype(jnp.float32) + got.astype(jnp.float32)).astype(jnp.bfloat16)
    total = chip.astype(jnp.float32)
    for step in range(1, lax.axis_size("narrow") // 2):
        total = total + shifted(chip, "narrow", 2 * step).astype(jnp.float32)
    return total


def both_halves(mine, is_odd):
    other = from_partner(mine)
    return jnp.concatenate(
        [jnp.where(is_odd, other, mine), jnp.where(is_odd, mine, other)], axis=1
    )


def gather_wide(rows):
    wide = lax.axis_size("wide")
    return jnp.concatenate([rows] + [shifted(rows, "wide", j) for j in range(1, wide)], axis=0)


def scatter_wide(part, own_rows):
    wide = lax.axis_size("wide")
    rows = part.shape[0] // wide
    total = own_rows.astype(jnp.float32) + part[:rows].astype(jnp.float32)
    for j in range(1, wide):
        block = part[j * rows : (j + 1) * rows]
        total = total + shifted(block, "wide", -j).astype(jnp.float32)
    return total.astype(jnp.bfloat16)


def body(saved_inputs, upstream, up_weight, down_weight):
    w_up = up_weight[0]
    w_down = down_weight[0]
    wide = lax.axis_size("wide")
    place = lax.axis_index("wide")
    is_odd = lax.axis_index("narrow") % 2 == 1
    is_upper = lax.axis_index("section") == 1
    tokens, width = saved_inputs.shape[1:]
    rows = min(CHUNK_ROWS, tokens // wide)
    chunks = tokens // wide // rows

    blocks = saved_inputs[0].reshape(wide, chunks, rows, width)
    blocks = [
        lax.dynamic_index_in_dim(blocks, lax.rem(place + wide - j, wide), 0, keepdims=False)
        for j in range(wide)
    ]
    saved = [
        jnp.concatenate([block[c] for block in blocks], axis=0) for c in range(chunks)
    ]
    own = [upstream[c * rows : (c + 1) * rows] for c in range(chunks)]

    def backward(incoming, own_rows, slopes):
        back = sum_half(contract_cols(incoming, w_down).astype(jnp.bfloat16), is_odd)
        slope = both_halves((back * slopes).astype(jnp.bfloat16), is_odd)
        part = contract_cols(slope, w_up).astype(jnp.bfloat16)
        return slope, scatter_wide(part, own_rows)

    hidden, slopes, second = [], [], []
    for c in range(chunks):
        first_in = gather_wide(own[c])
        part = jnp.dot(saved[c], w_up, preferred_element_type=jnp.float32).astype(jnp.bfloat16)
        act, slope_of = gelu_parts(sum_half(part, is_odd))
        hidden.append(both_halves(act.astype(jnp.bfloat16), is_odd))
        slopes.append(slope_of)
        _, grad = backward(first_in, own[c], slope_of)
        second.append(lax.ppermute(grad, "section", [(1, 0)]))
    incoming, slope, grads = [], [], []
    for c in range(chunks):
        own_rows = jnp.where(is_upper, own[c], second[c])
        incoming.append(gather_wide(own_rows))
        one_slope, grad = backward(incoming[c], own_rows, slopes[c])
        slope.append(one_slope)
        grads.append(grad)
    grad_down = contract_rows(
        jnp.concatenate(hidden, axis=0), jnp.concatenate(incoming, axis=0)
    ).astype(jnp.bfloat16)
    grad_up = contract_rows(
        jnp.concatenate(saved, axis=0), jnp.concatenate(slope, axis=0)
    ).astype(jnp.bfloat16)
    return jnp.concatenate(grads, axis=0)[None], grad_up[None], grad_down[None]


def solution(mesh):
    placed = (
        P("section", None, "narrow"),
        P("wide", "narrow"),
        P("section", "narrow", "wide"),
        P("section", "wide", "narrow"),
    )
    return jax.shard_map(
        body,
        mesh=mesh,
        in_specs=placed,
        out_specs=(
            P("section", "wide", "narrow"),
            P("section", "narrow", "wide"),
            P("section", "wide", "narrow"),
        ),
        check_vma=False,
    )
```

```python
import jax
import jax.numpy as jnp
from jax import lax
from jax.experimental.layout import Layout, with_layout_constraint
from jax.sharding import PartitionSpec as P

gelu_scale = 0.7978845608028654
cubic_term = 0.044715
CHUNK_ROWS = 64


def shifted(block, axis, distance):
    size = lax.axis_size(axis)
    return lax.ppermute(block, axis, [(i, (i + distance) % size) for i in range(size)])


def from_partner(block):
    size = lax.axis_size("narrow")
    return lax.ppermute(block, "narrow", [(i, i ^ 1) for i in range(size)])


def gelu_parts(pre_act):
    inner = jnp.tanh(gelu_scale * (pre_act + cubic_term * pre_act * pre_act * pre_act))
    act_value = 0.5 * pre_act * (1.0 + inner)
    slopes = 0.5 * (1.0 + inner) + 0.5 * pre_act * (1.0 - inner * inner) * gelu_scale * (
        1.0 + 3.0 * cubic_term * pre_act * pre_act
    )
    return (act_value, slopes)


def contract(first_op, second_op, dims):
    return lax.dot_general(
        first_op, second_op, ((dims[:1], dims[1:]), ((), ())), preferred_element_type=jnp.float32
    )


def row_major(block):
    return with_layout_constraint(block, Layout(major_to_minor=(0, 1)))


def turned(block):
    return row_major(block.T)


def sum_half(part, axis, is_odd):
    low, high = jnp.split(part, 2, axis=axis)
    got = from_partner(jnp.where(is_odd, low, high))
    mine = jnp.where(is_odd, high, low)
    chip = (mine.astype(jnp.float32) + got.astype(jnp.float32)).astype(jnp.bfloat16)
    total = chip.astype(jnp.float32)
    for step in range(1, lax.axis_size("narrow") // 2):
        total = total + shifted(chip, "narrow", 2 * step).astype(jnp.float32)
    return total


def both_halves(mine, axis, is_odd):
    other = from_partner(mine)
    return jnp.concatenate(
        [jnp.where(is_odd, other, mine), jnp.where(is_odd, mine, other)], axis=axis
    )


def wide_masks():
    size = lax.axis_size("wide")
    return [1 << bit for bit in range(size.bit_length() - 1)]


def from_place(block, mask):
    return lax.ppermute(
        block, "wide", [(i, i ^ mask) for i in range(lax.axis_size("wide"))]
    )


def block_order():
    order = [0]
    for mask in reversed(wide_masks()):
        order = order + [j ^ mask for j in order]
    return order


def gather_wide(rows):
    for mask in reversed(wide_masks()):
        rows = jnp.concatenate([rows, from_place(rows, mask)], axis=0)
    return rows


def scatter_wide(part, own_rows):
    for mask in wide_masks():
        keep, send = jnp.split(part, 2, axis=0)
        total = keep.astype(jnp.float32) + from_place(send, mask).astype(jnp.float32)
        part = total.astype(jnp.bfloat16)
    return (own_rows.astype(jnp.float32) + total).astype(jnp.bfloat16)


def body(saved_inputs, upstream, up_weight, down_weight):
    w_up = up_weight[0]
    w_down = down_weight[0]
    wide = lax.axis_size("wide")
    place = lax.axis_index("wide")
    is_odd = lax.axis_index("narrow") % 2 == 1
    is_upper = lax.axis_index("section") == 1
    tokens, width = saved_inputs.shape[1:]
    rows = min(CHUNK_ROWS, tokens // wide)
    chunks = tokens // wide // rows

    blocks = saved_inputs[0].reshape(wide, chunks, rows, width)
    blocks = [
        lax.dynamic_index_in_dim(blocks, jnp.bitwise_xor(place, j), 0, keepdims=False)
        for j in block_order()
    ]
    saved = [
        jnp.concatenate([block[c] for block in blocks], axis=0) for c in range(chunks)
    ]
    own = [upstream[c * rows : (c + 1) * rows] for c in range(chunks)]

    def backward(incoming, own_rows, slopes):
        part = row_major(contract(w_down, turned(incoming), (1, 0)).astype(jnp.bfloat16))
        back = sum_half(part, 0, is_odd)
        slope = row_major(both_halves((back * slopes).astype(jnp.bfloat16), 0, is_odd))
        part = row_major(contract(w_up, slope, (1, 0)).astype(jnp.bfloat16))
        return slope, scatter_wide(turned(part), own_rows)

    hidden, slopes, second = [], [], []
    for c in range(chunks):
        first_in = gather_wide(own[c])
        part = contract(saved[c], w_up, (1, 0)).astype(jnp.bfloat16)
        act, slope_of = gelu_parts(sum_half(part, 1, is_odd))
        hidden.append(both_halves(act.astype(jnp.bfloat16), 1, is_odd))
        slopes.append(turned(slope_of))
        _, grad = backward(first_in, own[c], slopes[c])
        second.append(lax.ppermute(grad, "section", [(1, 0)]))
    incoming, slope, grads = [], [], []
    for c in range(chunks):
        own_rows = jnp.where(is_upper, own[c], second[c])
        incoming.append(gather_wide(own_rows))
        one_slope, grad = backward(incoming[c], own_rows, slopes[c])
        slope.append(one_slope)
        grads.append(grad)
    grad_down = contract(
        jnp.concatenate(hidden, axis=0), jnp.concatenate(incoming, axis=0), (0, 0)
    ).astype(jnp.bfloat16)
    grad_up = contract(
        jnp.concatenate(saved, axis=0), jnp.concatenate(slope, axis=1), (0, 1)
    ).astype(jnp.bfloat16)
    return jnp.concatenate(grads, axis=0)[None], grad_up[None], grad_down[None]


def solution(mesh):
    placed = (
        P("section", None, "narrow"),
        P("wide", "narrow"),
        P("section", "narrow", "wide"),
        P("section", "wide", "narrow"),
    )
    return jax.shard_map(
        body,
        mesh=mesh,
        in_specs=placed,
        out_specs=(
            P("section", "wide", "narrow"),
            P("section", "narrow", "wide"),
            P("section", "wide", "narrow"),
        ),
        check_vma=False,
    )
```

```python
import jax
import jax.numpy as jnp
from jax import lax
from jax.experimental import pallas as pl
from jax.experimental.pallas import tpu as pltpu
from jax.sharding import PartitionSpec as P

gelu_scale = 0.7978845608028654
cubic_term = 0.044715
CHUNK_ROWS = 64


def shifted(block, axis, distance):
    size = lax.axis_size(axis)
    return lax.ppermute(block, axis, [(i, (i + distance) % size) for i in range(size)])


def from_partner(block):
    size = lax.axis_size("narrow")
    return lax.ppermute(block, "narrow", [(i, i ^ 1) for i in range(size)])


def gelu_parts(pre_act):
    inner = jnp.tanh(gelu_scale * (pre_act + cubic_term * pre_act * pre_act * pre_act))
    act_value = 0.5 * pre_act * (1.0 + inner)
    slopes = 0.5 * (1.0 + inner) + 0.5 * pre_act * (1.0 - inner * inner) * gelu_scale * (
        1.0 + 3.0 * cubic_term * pre_act * pre_act
    )
    return (act_value, slopes)


def contract(first_op, second_op, dims):
    return lax.dot_general(
        first_op, second_op, ((dims[:1], dims[1:]), ((), ())), preferred_element_type=jnp.float32
    )


def product_kernel(first_ref, second_ref, out_ref):
    out_ref[...] = jnp.dot(
        first_ref[...], second_ref[...], preferred_element_type=jnp.float32
    ).astype(out_ref.dtype)


def product(first_op, second_op, stream_first):
    rows, depth = first_op.shape
    columns = second_op.shape[1]
    if stream_first:
        block = min(512, rows)
        grid = (rows // block,)
        in_specs = [
            pl.BlockSpec((block, depth), lambda i: (i, 0)),
            pl.BlockSpec((depth, columns), lambda i: (0, 0)),
        ]
        out_spec = pl.BlockSpec((block, columns), lambda i: (i, 0))
    else:
        block = min(512, columns)
        grid = (columns // block,)
        in_specs = [
            pl.BlockSpec((rows, depth), lambda i: (0, 0)),
            pl.BlockSpec((depth, block), lambda i: (0, i)),
        ]
        out_spec = pl.BlockSpec((rows, block), lambda i: (0, i))
    return pl.pallas_call(
        product_kernel,
        grid=grid,
        in_specs=in_specs,
        out_specs=out_spec,
        out_shape=jax.ShapeDtypeStruct((rows, columns), jnp.bfloat16),
        compiler_params=pltpu.CompilerParams(vmem_limit_bytes=28 * 2**20),
        cost_estimate=pl.CostEstimate(
            flops=2 * rows * depth * columns,
            bytes_accessed=2 * (rows * depth + depth * columns + rows * columns),
            transcendentals=0,
        ),
    )(first_op, second_op)


def turned(block):
    return lax.optimization_barrier(block.T)


def chip_half(part, axis, is_odd):
    low, high = jnp.split(part, 2, axis=axis)
    got = from_partner(jnp.where(is_odd, low, high))
    mine = jnp.where(is_odd, high, low)
    return (mine.astype(jnp.float32) + got.astype(jnp.float32)).astype(jnp.bfloat16)


def sum_chips(chip):
    total = chip.astype(jnp.float32)
    for step in range(1, lax.axis_size("narrow") // 2):
        total = total + shifted(chip, "narrow", 2 * step).astype(jnp.float32)
    return total


def both_halves(mine, axis, is_odd):
    other = from_partner(mine)
    return jnp.concatenate(
        [jnp.where(is_odd, other, mine), jnp.where(is_odd, mine, other)], axis=axis
    )


def wide_masks():
    size = lax.axis_size("wide")
    return [1 << bit for bit in range(size.bit_length() - 1)]


def from_place(block, mask):
    return lax.ppermute(
        block, "wide", [(i, i ^ mask) for i in range(lax.axis_size("wide"))]
    )


def block_order():
    order = [0]
    for mask in reversed(wide_masks()):
        order = order + [j ^ mask for j in order]
    return order


def gather_wide(rows):
    for mask in reversed(wide_masks()):
        rows = jnp.concatenate([rows, from_place(rows, mask)], axis=0)
    return rows


def scatter_wide(part, own_rows):
    for mask in wide_masks():
        keep, send = jnp.split(part, 2, axis=0)
        total = keep.astype(jnp.float32) + from_place(send, mask).astype(jnp.float32)
        part = total.astype(jnp.bfloat16)
    return (own_rows.astype(jnp.float32) + total).astype(jnp.bfloat16)


def body(saved_inputs, upstream, up_weight, down_weight):
    w_up = up_weight[0]
    w_down = down_weight[0]
    wide = lax.axis_size("wide")
    place = lax.axis_index("wide")
    is_odd = lax.axis_index("narrow") % 2 == 1
    is_upper = lax.axis_index("section") == 1
    tokens, width = saved_inputs.shape[1:]
    rows = min(CHUNK_ROWS, tokens // wide)
    chunks = tokens // wide // rows

    blocks = saved_inputs[0].reshape(wide, chunks, rows, width)
    blocks = [
        lax.dynamic_index_in_dim(blocks, jnp.bitwise_xor(place, j), 0, keepdims=False)
        for j in block_order()
    ]
    saved = [
        jnp.concatenate([block[c] for block in blocks], axis=0) for c in range(chunks)
    ]
    own = [upstream[c * rows : (c + 1) * rows] for c in range(chunks)]

    def back_chip(incoming):
        return chip_half(product(w_down, turned(incoming), True), 0, is_odd)

    def onward(back, own_rows, slopes):
        slope = both_halves((back * slopes).astype(jnp.bfloat16), 0, is_odd)
        part = product(w_up, slope, True)
        return slope, scatter_wide(turned(part), own_rows)

    first_in = [gather_wide(own[c]) for c in range(chunks)]
    chips = [chip_half(product(saved[c], w_up, False), 1, is_odd) for c in range(chunks)]
    hidden, slopes, second = [], [], []
    for c in range(chunks):
        act, slope_of = gelu_parts(sum_chips(chips[c]))
        hidden.append(act.astype(jnp.bfloat16))
        slope_of, first_in[c] = lax.optimization_barrier((slope_of.T, first_in[c]))
        slopes.append(slope_of)
    chips = [back_chip(first_in[c]) for c in range(chunks)]
    for c in range(chunks):
        _, grad = onward(sum_chips(chips[c]), own[c], slopes[c])
        second.append(lax.ppermute(grad, "section", [(1, 0)]))
    hidden = [both_halves(one, 1, is_odd) for one in hidden]
    own = [jnp.where(is_upper, own[c], second[c]) for c in range(chunks)]
    incoming = [gather_wide(own[c]) for c in range(chunks)]
    chips = [back_chip(incoming[c]) for c in range(chunks)]
    back = [sum_chips(one) for one in chips]
    all_hidden, _ = lax.optimization_barrier((jnp.concatenate(hidden, axis=0), chips[-1]))
    grad_down = contract(all_hidden, jnp.concatenate(incoming, axis=0), (0, 0)).astype(
        jnp.bfloat16
    )
    grad_down, back[0] = lax.optimization_barrier((grad_down, back[0]))
    slope, grads = [], []
    for c in range(chunks):
        one_slope, grad = onward(back[c], own[c], slopes[c])
        slope.append(one_slope)
        grads.append(grad)
    grad_up = contract(
        jnp.concatenate(saved, axis=0), jnp.concatenate(slope, axis=1), (0, 1)
    ).astype(jnp.bfloat16)
    return jnp.concatenate(grads, axis=0)[None], grad_up[None], grad_down[None]


def solution(mesh):
    placed = (
        P("section", None, "narrow"),
        P("wide", "narrow"),
        P("section", "narrow", "wide"),
        P("section", "wide", "narrow"),
    )
    return jax.shard_map(
        body,
        mesh=mesh,
        in_specs=placed,
        out_specs=(
            P("section", "wide", "narrow"),
            P("section", "narrow", "wide"),
            P("section", "wide", "narrow"),
        ),
        check_vma=False,
    )
```

```python
import jax
import jax.numpy as jnp
from jax import lax
from jax.experimental import pallas as pl
from jax.experimental.pallas import tpu as pltpu
from jax.sharding import PartitionSpec as P

gelu_scale = 0.7978845608028654
cubic_term = 0.044715
CHUNK_ROWS = 64


def shifted(block, axis, distance):
    size = lax.axis_size(axis)
    return lax.ppermute(block, axis, [(i, (i + distance) % size) for i in range(size)])


def from_partner(block):
    size = lax.axis_size("narrow")
    return lax.ppermute(block, "narrow", [(i, i ^ 1) for i in range(size)])


def gelu_parts(pre_act):
    inner = jnp.tanh(gelu_scale * (pre_act + cubic_term * pre_act * pre_act * pre_act))
    act_value = 0.5 * pre_act * (1.0 + inner)
    slopes = 0.5 * (1.0 + inner) + 0.5 * pre_act * (1.0 - inner * inner) * gelu_scale * (
        1.0 + 3.0 * cubic_term * pre_act * pre_act
    )
    return (act_value, slopes)


def contract(first_op, second_op, dims):
    return lax.dot_general(
        first_op, second_op, ((dims[:1], dims[1:]), ((), ())), preferred_element_type=jnp.float32
    )


def product_kernel(first_ref, second_ref, out_ref):
    out_ref[...] = jnp.dot(
        first_ref[...], second_ref[...], preferred_element_type=jnp.float32
    ).astype(out_ref.dtype)


def product(first_op, second_op, stream_first):
    rows, depth = first_op.shape
    columns = second_op.shape[1]
    if stream_first:
        block = min(512, rows)
        grid = (rows // block,)
        in_specs = [
            pl.BlockSpec((block, depth), lambda i: (i, 0)),
            pl.BlockSpec((depth, columns), lambda i: (0, 0)),
        ]
        out_spec = pl.BlockSpec((block, columns), lambda i: (i, 0))
    else:
        block = min(512, columns)
        grid = (columns // block,)
        in_specs = [
            pl.BlockSpec((rows, depth), lambda i: (0, 0)),
            pl.BlockSpec((depth, block), lambda i: (0, i)),
        ]
        out_spec = pl.BlockSpec((rows, block), lambda i: (0, i))
    return pl.pallas_call(
        product_kernel,
        grid=grid,
        in_specs=in_specs,
        out_specs=out_spec,
        out_shape=jax.ShapeDtypeStruct((rows, columns), jnp.bfloat16),
        compiler_params=pltpu.CompilerParams(vmem_limit_bytes=48 * 2**20),
        cost_estimate=pl.CostEstimate(
            flops=2 * rows * depth * columns,
            bytes_accessed=2 * (rows * depth + depth * columns + rows * columns),
            transcendentals=0,
        ),
    )(first_op, second_op)


def turned(block):
    return lax.optimization_barrier(block.T)


def chip_half(part, axis, is_odd):
    low, high = jnp.split(part, 2, axis=axis)
    got = from_partner(jnp.where(is_odd, low, high))
    mine = jnp.where(is_odd, high, low)
    return (mine.astype(jnp.float32) + got.astype(jnp.float32)).astype(jnp.bfloat16)


def sum_chips(chip):
    total = chip.astype(jnp.float32)
    for step in range(1, lax.axis_size("narrow") // 2):
        total = total + shifted(chip, "narrow", 2 * step).astype(jnp.float32)
    return total


def both_halves(mine, axis, is_odd):
    other = from_partner(mine)
    return jnp.concatenate(
        [jnp.where(is_odd, other, mine), jnp.where(is_odd, mine, other)], axis=axis
    )


def wide_masks():
    size = lax.axis_size("wide")
    return [1 << bit for bit in range(size.bit_length() - 1)]


def from_place(block, mask):
    return lax.ppermute(
        block, "wide", [(i, i ^ mask) for i in range(lax.axis_size("wide"))]
    )


def block_order():
    order = [0]
    for mask in reversed(wide_masks()):
        order = order + [j ^ mask for j in order]
    return order


def gather_wide(rows):
    for mask in reversed(wide_masks()):
        rows = jnp.concatenate([rows, from_place(rows, mask)], axis=0)
    return rows


def scatter_wide(part, own_rows):
    for mask in wide_masks():
        keep, send = jnp.split(part, 2, axis=0)
        total = keep.astype(jnp.float32) + from_place(send, mask).astype(jnp.float32)
        part = total.astype(jnp.bfloat16)
    return (own_rows.astype(jnp.float32) + total).astype(jnp.bfloat16)


def body(saved_inputs, upstream, up_weight, down_weight):
    w_up = up_weight[0]
    w_down = down_weight[0]
    wide = lax.axis_size("wide")
    place = lax.axis_index("wide")
    is_odd = lax.axis_index("narrow") % 2 == 1
    is_upper = lax.axis_index("section") == 1
    tokens, width = saved_inputs.shape[1:]
    rows = min(CHUNK_ROWS, tokens // wide)
    chunks = tokens // wide // rows

    blocks = saved_inputs[0].reshape(wide, chunks, rows, width)
    blocks = [
        lax.dynamic_index_in_dim(blocks, jnp.bitwise_xor(place, j), 0, keepdims=False)
        for j in block_order()
    ]
    saved = [
        jnp.concatenate([block[c] for block in blocks], axis=0) for c in range(chunks)
    ]
    own = [upstream[c * rows : (c + 1) * rows] for c in range(chunks)]

    def back_chip(incoming):
        return chip_half(product(w_down, turned(incoming), True), 0, is_odd)

    def onward(back, own_rows, slopes):
        slope = both_halves((back * slopes).astype(jnp.bfloat16), 0, is_odd)
        part = product(w_up, slope, True)
        return slope, scatter_wide(turned(part), own_rows)

    first_in = [gather_wide(own[c]) for c in range(chunks)]
    chips = [chip_half(product(saved[c], w_up, False), 1, is_odd) for c in range(chunks)]
    hidden, slopes, second = [], [], []
    for c in range(chunks):
        act, slope_of = gelu_parts(sum_chips(chips[c]))
        hidden.append(act.astype(jnp.bfloat16))
        slope_of, first_in[c] = lax.optimization_barrier((slope_of.T, first_in[c]))
        slopes.append(slope_of)
    chips = [back_chip(first_in[c]) for c in range(chunks)]
    for c in range(chunks):
        _, grad = onward(sum_chips(chips[c]), own[c], slopes[c])
        second.append(lax.ppermute(grad, "section", [(1, 0)]))
    hidden = [both_halves(one, 1, is_odd) for one in hidden]
    own = [jnp.where(is_upper, own[c], second[c]) for c in range(chunks)]
    incoming = [gather_wide(own[c]) for c in range(chunks)]
    chips = [back_chip(incoming[c]) for c in range(chunks)]
    back = [sum_chips(one) for one in chips]
    grad_down = contract(
        jnp.concatenate(hidden, axis=0), jnp.concatenate(incoming, axis=0), (0, 0)
    ).astype(jnp.bfloat16)
    slope, grads = [], []
    for c in range(chunks):
        one_slope, grad = onward(back[c], own[c], slopes[c])
        slope.append(one_slope)
        grads.append(grad)
    grad_up = contract(
        jnp.concatenate(saved, axis=0), jnp.concatenate(slope, axis=1), (0, 1)
    ).astype(jnp.bfloat16)
    return jnp.concatenate(grads, axis=0)[None], grad_up[None], grad_down[None]


def solution(mesh):
    placed = (
        P("section", None, "narrow"),
        P("wide", "narrow"),
        P("section", "narrow", "wide"),
        P("section", "wide", "narrow"),
    )
    return jax.shard_map(
        body,
        mesh=mesh,
        in_specs=placed,
        out_specs=(
            P("section", "wide", "narrow"),
            P("section", "narrow", "wide"),
            P("section", "wide", "narrow"),
        ),
        check_vma=False,
    )
```
